32 devices in a mesh: gx: 4 (over y, x), gy: 8 (over z, core).
Axes of the slice: x: 2, y: 2, z: 4, core: 2. Of those that a mesh axis runs over, the one named last changes fastest.
Arguments:
- images: bfloat16 [64, 2, 512, 512], P('gy', None, 'gx'), may hold values from -192 to 192
- rates: float32 [256], replicated, may hold values from 0.002 to 0.2
- smoothing: float32 [256], replicated, may hold values from 0.02 to 1
Outputs:
- spectra: float32 [2, 512, 512, 256], P(None, 'gx', 'gy')
The draws below stay inside these ranges and needn't reach their ends.
All inputs are finite; a program needn't handle non-finite values.
Results may differ from the reference program's by a relative error of at most 0.0033.
Values may be sent and summed in bfloat16 or wider, within the bound.
No kernel may reach another device: no remote copies, remote signals or barrier semaphores. Data moves between devices by JAX's collectives and lax.ppermute only.
A program may use at most 192 MiB of HBM per device.

```python
import math
import jax
import jax.numpy as jnp
from jax import lax

E = 64
R = 256
SL = 2
ITERS = 3
H = 512
W = 512


def draw_rates(key, part):
    spread_count = max(2, R // 32)
    low_log = math.log(0.002)
    mid_log = math.log(0.1)
    high_log = math.log(0.2)
    width = (mid_log - low_log) / spread_count
    first_key = jax.random.fold_in(key, 11)
    second_key = jax.random.fold_in(key, 23)
    third_key = jax.random.fold_in(key, 37)
    offsets = jax.random.uniform(first_key, (spread_count,), dtype=jnp.float32)
    spread_logs = low_log + width * (jnp.arange(spread_count, dtype=jnp.float32) + offsets)
    dense_logs = jax.random.uniform(second_key, (R - spread_count,), dtype=jnp.float32, minval=mid_log, maxval=high_log)
    all_logs = jnp.concatenate([spread_logs, dense_logs])
    order = jax.random.permutation(third_key, R)
    return jnp.exp(all_logs[order]).astype(jnp.float32)


def shard_levels(own_key, shape, cuts, low, high):
    loudness = 1.0
    for axis_at, shards_of in cuts:
        steps = jax.random.uniform(jax.random.fold_in(jax.random.fold_in(own_key, 6), axis_at), (shards_of,), jnp.float32, low / len(cuts), high / len(cuts))
        loudness = loudness * jnp.repeat(jnp.exp(steps), shape[axis_at] // shards_of).reshape((-1,) + (1,) * (len(shape) - 1 - axis_at))
    return loudness


def scatter_about(key, shape, scale, reach, split=(), kind=jnp.bfloat16):
    values = scale * jax.random.normal(key, shape, jnp.float32)
    if split:
        values = values * shard_levels(key, shape, split, -0.22, 0.18)
    return jnp.clip(values, -reach, reach).astype(kind)


def setup_inputs(seed: int = 0) -> dict:
    streams_of = jax.random.split(jax.random.key(seed), 4)
    return {
        "images": scatter_about(streams_of[0], (E, SL, H, W), 32.0, 192.0, ((0, 8), (2, 4))),
        "rates": draw_rates(jax.random.fold_in(streams_of[3], 71), 0),
        "smoothing": jnp.clip(jnp.exp(jax.random.uniform(streams_of[2], (R,), jnp.float32, math.log(0.02), math.log(1.0))), 0.02, 1.0),
    }


def kernel_parts(rates, smoothing):
    times = 10.0 * (jnp.arange(E, dtype=jnp.float32) + 1.0)
    raw = jnp.exp(-times[:, None] * rates[None, :])
    kernel = raw / jnp.sqrt(lax.optimization_barrier(jnp.sum(raw * raw, axis=0)))[None, :]
    gram = jnp.dot(kernel.T, kernel, precision=lax.Precision.HIGHEST)
    rowsum = lax.optimization_barrier(jnp.sum(gram, axis=1))
    lam = smoothing * rowsum
    step = 1.0 / (rowsum + 8.0 * lam)
    return (kernel, gram, lam, step)

def laplace(field):
    padded = jnp.pad(field, ((1, 1), (1, 1), (0, 0)))
    center = padded[1:-1, 1:-1]
    return 4.0 * center - padded[2:, 1:-1] - padded[:-2, 1:-1] - padded[1:-1, 2:] - padded[1:-1, :-2]

def reference(images, rates, smoothing):
    kernel, gram, lam, step = kernel_parts(rates, smoothing)
    kernel_b = kernel.astype(jnp.bfloat16).astype(jnp.float32)

    def one_slice(slab):
        rows, cols = (slab.shape[1], slab.shape[2])
        proj = jnp.einsum('eij,er->ijr', slab.astype(jnp.float32), kernel_b, precision=lax.Precision.HIGHEST)
        field = jnp.maximum(proj * step, 0.0)
        for count in range(ITERS - 1):
            curved = jnp.dot(field.reshape(rows * cols, R), gram, precision=lax.Precision.HIGHEST).reshape(rows, cols, R)
            grad = curved - proj + lam * laplace(field)
            field = jnp.maximum(field - step * grad, 0.0)
        return field
    return lax.map(one_slice, jnp.transpose(images, (1, 0, 2, 3)))
```

```python
import functools

import jax
import jax.numpy as jnp
from jax import lax
from jax.experimental import pallas as pl
from jax.experimental.pallas import tpu as pltpu
from jax.sharding import PartitionSpec as P

E = 64
BLK = 16
LANES = 128
HALF = 64
ORDER = (0, 4, 1, 5, 2, 6, 3, 7)
RB = 4
TURN = 16
PACK_VMEM, FIT_VMEM = 63 * 2**20, 63 * 2**20

CHUNKS = ((2, 3, 4), (5, 6, 7, 8), (0, 1, -1))
SEGS = ((36, 76, 1), (76, 128, 2), (0, 36, 3))


def parts_body(echoes, place, rates, smoothing, _, kb_ref, gs_ref, vec_ref):
    chip, core = place[0], place[1]
    pos = lax.broadcasted_iota(jnp.int32, (E, 1), 0)
    raw = jnp.exp(-10.0 * (pos.astype(jnp.float32) + 1.0) * rates[...])
    norm = jnp.sqrt(jnp.sum(raw * raw, axis=0, keepdims=True))
    kernel = raw / norm
    gram = lax.dot_general(
        kernel,
        kernel,
        (((0,), (0,)), ((), ())),
        precision=lax.Precision.HIGHEST,
        preferred_element_type=jnp.float32,
    )
    rowsum = jnp.sum(gram, axis=0, keepdims=True)
    lam = smoothing[...] * rowsum
    step = 1.0 / (rowsum + 8.0 * lam)
    owner = 2 * (chip ^ (pos // (2 * echoes))) + (core ^ (pos // echoes % 2))
    times = 10.0 * ((owner * echoes + pos % echoes).astype(jnp.float32) + 1.0)
    kb_ref[...] = (jnp.exp(-times * rates[...]) / norm).astype(jnp.bfloat16)
    gs_ref[...] = (gram * step).astype(jnp.bfloat16)
    pull = step * lam
    vec_ref[0:1, :] = step
    vec_ref[1:2, :] = 1.0 - 4.0 * pull
    vec_ref[2:3, :] = pull


def kernel_parts(rates, smoothing, place, echoes, later):
    bins = rates.shape[0]
    whole = pl.BlockSpec(memory_space=pltpu.VMEM)
    return pl.pallas_call(
        functools.partial(parts_body, echoes),
        out_shape=[
            jax.ShapeDtypeStruct((E, bins), jnp.bfloat16),
            jax.ShapeDtypeStruct((bins, bins), jnp.bfloat16),
            jax.ShapeDtypeStruct((8, bins), jnp.float32),
        ],
        in_specs=[pl.BlockSpec(memory_space=pltpu.SMEM), whole, whole, pl.BlockSpec(memory_space=pl.ANY)],
        out_specs=[whole] * 3,
        compiler_params=pltpu.CompilerParams(vmem_limit_bytes=PACK_VMEM),
        name="parts",
    )(place, rates[None, :], smoothing[None, :], later)


def pack_body(chips, count, ends, place, *refs):
    ins, refs = refs[: 2 * count], refs[2 * count :]
    ends, outs, turned = refs[:ends], refs[ends:-1], refs[-1]
    echoes = ins[0].shape[0]
    chip, core = place[0], place[1]
    if ends:
        for p in range(2):
            outs[chips][p * echoes : (p + 1) * echoes] = ends[p][:, :, 0:2]
            outs[chips + 1][p * echoes : (p + 1) * echoes] = ends[2 + p][:, :, BLK - 2 : BLK]
    lane = lax.broadcasted_iota(jnp.int32, (2 * echoes, LANES), 1)
    in_place = (lane < HALF) == (core == 0)
    moved_lane = (lane + HALF * core) % LANES
    from_left = moved_lane >= LANES - 2
    holds = jnp.where(lane % 4 < 2, moved_lane // 4, (moved_lane // 4 + 16) % 32)
    top = 0
    for n in range(count):
        height = ins[2 * n].shape[2]
        for p in range(2):
            for e in range(echoes):
                for s in range(2):
                    x = ins[2 * n + p][e, s].astype(jnp.float32)
                    for z in range(chips):
                        at = pl.ds(p * echoes + e, height, stride=2 * echoes)
                        turned[s, z, at, :] = x[:, z * LANES : (z + 1) * LANES]
        for k in range(chips):
            to = chip ^ k
            left_of, right_of = to - 1 + core, to + core
            has_left = (left_of >= 0).astype(jnp.float32)
            has_right = (right_of < chips).astype(jnp.float32)
            left_of, right_of = jnp.maximum(left_of, 0), jnp.minimum(right_of, chips - 1)
            edge = jnp.zeros((2 * echoes, LANES), jnp.float32)
            for r in range(height):
                at = pl.ds(r * 2 * echoes, 2 * echoes)
                moved = pltpu.roll(turned[1 - core, to, at, :], HALF, 1)
                outs[k][top + r] = jnp.where(in_place, turned[core, to, at, :], moved).astype(jnp.bfloat16)
                for s in range(2):
                    i = r + BLK * s
                    both = jnp.where(from_left, turned[s, left_of, at, :], turned[s, right_of, at, :])
                    edge = jnp.where(holds == i, pltpu.roll(both.astype(jnp.bfloat16), 4 * i + 2, 1).astype(jnp.float32), edge)
            edge = edge * jnp.where(lane % 4 < 2, has_left, has_right)
            outs[k][top + height] = pltpu.roll(edge, HALF * core, 1).astype(jnp.bfloat16)
        top += height + 1


def pack(pair, place, chunk, beyond, chips, edges):
    echoes, slices, height, cols = pair[0].shape
    block = lambda b: pl.BlockSpec((echoes, slices, BLK, cols), lambda _: (0, 0, b, 0))
    ins = [(a, block(b)) for b in chunk for a in pair]
    for a in beyond:
        half = lambda p: pl.BlockSpec((echoes,) + a.shape[1:], lambda _: (p, 0, 0, 0))
        ins += [(a, half(0)), (a, half(1))]
    count = len(ins) // 2
    rows = sum(spec.block_shape[2] + 1 for _, spec in ins[::2])
    shape = jax.ShapeDtypeStruct((rows, 2 * echoes, LANES), pair[0].dtype)
    out_shape = [shape] * chips
    extra = []
    if edges:
        extra = [(a, block(b)) for b in (0, height // BLK - 1) for a in pair]
        out_shape = out_shape + [jax.ShapeDtypeStruct((2 * echoes, slices, 2, cols), pair[0].dtype)] * 2
    ins = ins + extra
    zeros = lambda n: lambda _: (0,) * n
    return pl.pallas_call(
        functools.partial(pack_body, chips, count, len(extra)),
        grid=(1,),
        out_shape=out_shape,
        in_specs=[pl.BlockSpec(memory_space=pltpu.SMEM)] + [spec for _, spec in ins],
        out_specs=[pl.BlockSpec(o.shape, zeros(len(o.shape))) for o in out_shape],
        scratch_shapes=[pltpu.VMEM((2, chips, BLK * 2 * echoes, LANES), jnp.float32)],
        cost_estimate=pl.CostEstimate(
            flops=0, bytes_accessed=8 * echoes * slices * rows * cols, transcendentals=0
        ),
        compiler_params=pltpu.CompilerParams(vmem_limit_bytes=PACK_VMEM),
        name="pack",
    )(place, *[a for a, _ in ins])


def swap(a, axis, distance):
    count = lax.axis_size(axis)
    return lax.ppermute(a, axis, [(i, i ^ distance) for i in range(count)])


def even(count, most=RB):
    parts = pl.cdiv(count, most)
    at = [count * p // parts for p in range(parts + 1)]
    return [(a, b - a) for a, b in zip(at, at[1:])]


def fit_body(runs, counts, first, rows, ends, starts, place, kb_ref, gs_ref, vec_ref, *refs):
    total = sum(counts)
    arrays, out = refs[:total], refs[total + starts]
    lhs, lhs_h, turned, sb, v0b, w, v1b, sb_h, v0_h, lr_h, v1_h, result, sem = refs[total + starts + 1 :]
    sources, at = [], 0
    for n in counts:
        sources.append(arrays[at : at + n])
        at += n
    s = pl.program_id(0)
    at_left, at_right = (place[0] == 0) & (place[1] == 0), (place[0] == ends[0]) & (place[1] == 1)
    at_top, at_bottom = (place[2] == 0) & (first == 0), (place[2] == ends[1]) & (first + rows == out.shape[1])
    bins = gs_ref.shape[0]
    halves = [slice(0, LANES), slice(LANES, 2 * LANES)]
    main = slice(BLK, BLK + HALF)

    def gather(source, slot):
        return jnp.concatenate([ref[slot].astype(jnp.float32) for ref in source], axis=0)

    def turn(src, slot, to, u):
        turned[u, :, 0:E] = gather(src, slot).T
        for t in range(lhs.shape[0]):
            for k in range(HALF // BLK):
                pair = [turned[u, pl.ds(HALF * t + q, 8, stride=8), :][:, 0:E] for q in ORDER[2 * k : 2 * k + 2]]
                lhs[t, to, k * BLK : (k + 1) * BLK, :] = jnp.concatenate(pair, axis=0).astype(jnp.bfloat16)

    @pl.when(s == 0)
    def _():
        lhs_h[...] = jnp.zeros_like(lhs_h)
        for source, slot0, edge_slot, edge_row, to, length in runs:
            src = sources[source]
            full = length // TURN

            for t in range(length):
                turn(src, slot0 + t, to + t, t % TURN)
            turned[0, :, 0:E] = gather(src, edge_slot).T
            for t in range(lhs.shape[0]):
                i = BLK * t + edge_row
                for at, col in ((0, 4 * ((i + BLK) % 32) + 2), (1, 4 * ((i + BLK) % 32) + 3), (6, 4 * i), (7, 4 * i + 1)):
                    lhs_h[t, pl.ds(8 * to + at, length, stride=8), :] = turned[0, pl.ds(col, length, stride=4), :]

    step, keep, pull = vec_ref[0:1, :], vec_ref[1:2, :], vec_ref[2:3, :]
    sub = lax.broadcasted_iota(jnp.int32, (8, LANES), 0)

    def sides(v, outer):
        a, b = pltpu.roll(v[HALF - 8 :], 1, 0), pltpu.roll(v[0:8], 7, 0)
        c, d = pltpu.roll(outer, 1, 0), pltpu.roll(outer, 7, 0)
        left = jnp.concatenate([jnp.where(sub == 0, c, a), v[HALF - 16 : HALF - 8]], axis=0)
        right = jnp.concatenate([v[8:16], jnp.where(sub == 7, d, b)], axis=0)
        beside = jnp.where(sub == 0, a, b) + jnp.where(sub == 0, d, c)
        return left.astype(jnp.bfloat16), right.astype(jnp.bfloat16), beside

    x = lhs_h[s][:, 0:E].astype(jnp.bfloat16)
    b = jnp.dot(x, kb_ref[0:E], preferred_element_type=jnp.float32) * step
    sb_h[...] = b.reshape(rows + 4, 8, bins)
    v0_h[...] = jnp.maximum(b, 0.0).reshape(rows + 4, 8, bins)

    for j, height in even(rows + 4):
        x = lhs[s, j : j + height].reshape(height * HALF, E)
        b = jnp.dot(x, kb_ref[0:E], preferred_element_type=jnp.float32)
        for r in range(height):
            for h in halves:
                t = b[r * HALF : (r + 1) * HALF, h] * step[:, h]
                sb[j + r, :, h] = t
                v = jnp.maximum(t, 0.0)
                left, right, beside = sides(v, v0_h[j + r, :, h])
                v0b[j + r, 0:BLK, h] = left
                v0b[j + r, main, h] = v.astype(jnp.bfloat16)
                v0b[j + r, BLK + HALF :, h] = right
                lr_h[j + r, :, h] = beside

    x = v0_h[1 : rows + 3].astype(jnp.bfloat16).reshape((rows + 2) * 8, bins)
    g = jnp.dot(x, gs_ref[...], preferred_element_type=jnp.float32).reshape(rows + 2, 8, bins)
    at = lax.broadcasted_iota(jnp.int32, (1, 8, bins), 1)
    inside = jnp.where(((at == 0) & (at_right)) | ((at == 7) & at_left), 0.0, 1.0)
    near = lr_h[1 : rows + 3] + (v0_h[0 : rows + 2] + v0_h[2 : rows + 4])
    v = v0_h[1 : rows + 3] * keep + sb_h[1 : rows + 3] + pull * near - g
    v1_h[1 : rows + 3] = jnp.maximum(v, 0.0) * inside

    def around(ref, j, h):
        near = (ref[j, 0:HALF, h] + ref[j, 2 * BLK :, h]) + (ref[j - 1, main, h] + ref[j + 1, main, h])
        return near.astype(jnp.float32)

    for j, height in even(rows + 2):
        j += 1
        x = v0b[j : j + height, main].reshape(height * HALF, bins)
        g = jnp.dot(x, gs_ref[...], preferred_element_type=jnp.float32)
        for r in range(height):
            for h in halves:
                b = sb[j + r, :, h]
                near = around(v0b, j + r, h)
                v = jnp.maximum(b * (1.0 + keep[:, h]), b) + pull[:, h] * near - g[r * HALF : (r + 1) * HALF, h]
                v = jnp.maximum(v, 0.0)
                w[j + r, :, h] = v * keep[:, h] + b
                left, right, _unused = sides(v, v1_h[j + r, :, h])
                v1b[j + r, 0:BLK, h] = left
                v1b[j + r, main, h] = v.astype(jnp.bfloat16)
                v1b[j + r, BLK + HALF :, h] = right
    for outside, j in ((at_top, 1), (at_bottom, rows + 2)):

        @pl.when(outside)
        def _():
            v1b[j] = jnp.zeros_like(v1b[j])

    for i, height in even(rows):
        j = 2 + i
        x = v1b[j : j + height, main].reshape(height * HALF, bins)
        g = jnp.dot(x, gs_ref[...], preferred_element_type=jnp.float32)
        for r in range(height):
            for n, h in enumerate(halves):
                v = w[j + r, :, h] + pull[:, h] * around(v1b, j + r, h) - g[r * HALF : (r + 1) * HALF, h]
                v = jnp.maximum(v, 0.0)
                for t, q in enumerate(ORDER):
                    result[s, n, i + r, pl.ds(q, 8, stride=8), :] = v[8 * t : 8 * t + 8]
        for n, h in enumerate(halves):
            pltpu.make_async_copy(
                result.at[s, n, pl.ds(i, height)], out.at[s, pl.ds(first + i, height), :, h], sem.at[s]
            ).start()

    @pl.when(s == pl.num_programs(0) - 1)
    def _():
        for t in range(result.shape[0]):
            for n, h in enumerate(halves):
                pltpu.make_async_copy(result.at[t, n], out.at[t, pl.ds(first, rows), :, h], sem.at[t]).wait()


def fit(first, last, ends, shape, place, parts, sources, before):
    rows = last - first
    runs = []
    for to, row in enumerate(range(first - 2, last + 2)):
        for n, (_, where) in enumerate(sources):
            if row in where:
                slot, edge_slot, edge_row = where[row]
                prev = runs[-1] if runs else None
                if prev and prev[0] == n and prev[2] == edge_slot and prev[1] + prev[5] == slot:
                    runs[-1] = prev[:5] + (prev[5] + 1,)
                else:
                    runs.append((n, slot, edge_slot, edge_row, to, 1))
                break
        else:
            raise ValueError("row")
    keep = sorted({run[0] for run in runs})
    runs = [(keep.index(run[0]),) + run[1:] for run in runs]
    groups = [sources[n][0] for n in keep]
    arrays = [a for group in groups for a in group]
    counts = [len(group) for group in groups]
    slices = shape[0]
    whole = pl.BlockSpec(memory_space=pl.ANY)
    bins = shape[-1]
    tiles = lambda n, width, dtype: pltpu.VMEM((n, width, bins), dtype)
    specs = [pl.BlockSpec(a.shape, lambda s: (0, 0, 0)) for a in arrays]
    voxels = slices * rows * HALF
    started = [] if before is None else [before]
    return pl.pallas_call(
        functools.partial(fit_body, runs, counts, first, rows, ends, len(started)),
        grid=(slices,),
        out_shape=jax.ShapeDtypeStruct(shape, jnp.float32),
        in_specs=[pl.BlockSpec(memory_space=pltpu.SMEM)]
        + [pl.BlockSpec(p.shape, lambda s: (0, 0)) for p in parts]
        + specs
        + [whole] * len(started),
        out_specs=whole,
        scratch_shapes=[
            pltpu.VMEM((slices, rows + 4, HALF, E), jnp.bfloat16),
            pltpu.VMEM((slices, (rows + 4) * 8, LANES), jnp.float32),
            pltpu.VMEM((TURN, LANES, LANES), jnp.float32),
            tiles(rows + 4, HALF, jnp.float32),
            tiles(rows + 4, HALF + 2 * BLK, jnp.bfloat16),
            tiles(rows + 4, HALF, jnp.float32),
            tiles(rows + 4, HALF + 2 * BLK, jnp.bfloat16),
            tiles(rows + 4, 8, jnp.float32),
            tiles(rows + 4, 8, jnp.float32),
            tiles(rows + 4, 8, jnp.float32),
            tiles(rows + 4, 8, jnp.float32),
            pltpu.VMEM((slices, 2, rows, HALF, LANES), jnp.float32),
            pltpu.SemaphoreType.DMA((slices,)),
        ],
        input_output_aliases={4 + len(arrays): 0} if started else {},
        cost_estimate=pl.CostEstimate(
            flops=voxels * 256 * 2 * (2 * 256 + 64), bytes_accessed=voxels * 256 * 4, transcendentals=0
        ),
        compiler_params=pltpu.CompilerParams(vmem_limit_bytes=FIT_VMEM),
        name="fit",
    )(place, *parts, *arrays, *started)


def per_device(images, rates, smoothing):
    echoes, slices, height, _ = images.shape
    chips = lax.axis_size("gy") // 2
    ends = lax.axis_size("gx") - 1
    me = lax.axis_index("gy").astype(jnp.int32)
    place = jnp.stack([me // 2, me % 2, lax.axis_index("gx").astype(jnp.int32)])

    pair = (images, swap(images, "gy", 1))
    packs, wheres = [], []
    for n, chunk in enumerate(CHUNKS):
        inner = [b for b in chunk if 0 <= b < height // BLK]
        blocks = [[b * BLK + r for r in range(BLK)] for b in inner]
        extra = []
        if -1 in chunk:
            extra.append(above)
            blocks.append([-2, -1])
        if height // BLK in chunk:
            extra.append(below)
            blocks.append([height, height + 1])
        packed = pack(pair, place, inner, extra, chips, n == 0)
        if n == 0:
            top, bottom = packed[chips:]
            above = lax.ppermute(bottom, "gx", [(i, i + 1) for i in range(ends)])
            below = lax.ppermute(top, "gx", [(i + 1, i) for i in range(ends)])
            parts = kernel_parts(rates, smoothing, place, echoes, packed[0])
        packs.append(packed[:chips])
        where, at = {}, 0
        for block in blocks:
            for r, row in enumerate(block):
                where[row] = (at + r, at + len(block), r)
            at += len(block) + 1
        wheres.append(where)

    arrived = []
    for n in range(len(CHUNKS)):
        if n == 1:
            packs[1:], parts, arrived[0][1] = lax.optimization_barrier((packs[1:], parts, arrived[0][1]))
        elif n > 1:
            packs[n], arrived[n - 1] = lax.optimization_barrier((packs[n], arrived[n - 1]))
        moved = {k: swap(packs[n][k], "gy", 2 * k) for k in range(chips - 1, 0, -1)}
        arrived.append([packs[n][0]] + [moved[k] for k in range(1, chips)])

    shape = (slices, height, HALF, rates.shape[0])
    out = None
    for first, last, used in SEGS:
        out = fit(first, last, (chips - 1, ends), shape, place, parts, list(zip(arrived[:used], wheres)), out)
    return out


def solution(mesh):
    in_specs = (P("gy", None, "gx", None), P(), P())
    out_specs = P(None, "gx", "gy", None)
    return jax.shard_map(per_device, mesh=mesh, in_specs=in_specs, out_specs=out_specs, check_vma=False)
```

```python
import functools

import jax
import jax.numpy as jnp
from jax import lax
from jax.experimental import pallas as pl
from jax.experimental.pallas import tpu as pltpu
from jax.sharding import PartitionSpec as P

E = 64
BLK = 16
LANES = 128
HALF = 64
ORDER = (0, 4, 1, 5, 2, 6, 3, 7)
RB = 4
TURN = 16
PACK_VMEM, FIT_VMEM = 64 * 2**20, 64 * 2**20

CHUNKS = ((2, 3, 4), (5, 6, 7, 8), (0, 1, -1))
SEGS = ((36, 76, 1), (76, 128, 2), (0, 36, 3))


def parts_body(echoes, place, rates, smoothing, _, kb_ref, gs_ref, vec_ref):
    chip, core = place[0], place[1]
    pos = lax.broadcasted_iota(jnp.int32, (E, 1), 0)
    raw = jnp.exp(-10.0 * (pos.astype(jnp.float32) + 1.0) * rates[...])
    norm = jnp.sqrt(jnp.sum(raw * raw, axis=0, keepdims=True))
    kernel = raw / norm
    gram = lax.dot_general(
        kernel,
        kernel,
        (((0,), (0,)), ((), ())),
        precision=lax.Precision.HIGHEST,
        preferred_element_type=jnp.float32,
    )
    rowsum = jnp.sum(gram, axis=0, keepdims=True)
    lam = smoothing[...] * rowsum
    step = 1.0 / (rowsum + 8.0 * lam)
    owner = 2 * (chip ^ (pos // (2 * echoes))) + (core ^ (pos // echoes % 2))
    times = 10.0 * ((owner * echoes + pos % echoes).astype(jnp.float32) + 1.0)
    kb_ref[...] = (jnp.exp(-times * rates[...]) / norm).astype(jnp.bfloat16)
    gs_ref[...] = (gram * step).astype(jnp.bfloat16)
    pull = step * lam
    vec_ref[0:1, :] = step
    vec_ref[1:2, :] = 1.0 - 4.0 * pull
    vec_ref[2:3, :] = pull


def kernel_parts(rates, smoothing, place, echoes, later):
    bins = rates.shape[0]
    whole = pl.BlockSpec(memory_space=pltpu.VMEM)
    return pl.pallas_call(
        functools.partial(parts_body, echoes),
        out_shape=[
            jax.ShapeDtypeStruct((E, bins), jnp.bfloat16),
            jax.ShapeDtypeStruct((bins, bins), jnp.bfloat16),
            jax.ShapeDtypeStruct((8, bins), jnp.float32),
        ],
        in_specs=[pl.BlockSpec(memory_space=pltpu.SMEM), whole, whole, pl.BlockSpec(memory_space=pl.ANY)],
        out_specs=[whole] * 3,
        compiler_params=pltpu.CompilerParams(vmem_limit_bytes=PACK_VMEM),
        name="parts",
    )(place, rates[None, :], smoothing[None, :], later)


def pack_body(chips, count, ends, place, *refs):
    ins, refs = refs[: 2 * count], refs[2 * count :]
    ends, outs, turned = refs[:ends], refs[ends:-1], refs[-1]
    echoes = ins[0].shape[0]
    chip, core = place[0], place[1]
    if ends:
        for p in range(2):
            outs[chips][p * echoes : (p + 1) * echoes] = ends[p][:, :, 0:2]
            outs[chips + 1][p * echoes : (p + 1) * echoes] = ends[2 + p][:, :, BLK - 2 : BLK]
    lane = lax.broadcasted_iota(jnp.int32, (2 * echoes, LANES), 1)
    in_place = (lane < HALF) == (core == 0)
    moved_lane = (lane + HALF * core) % LANES
    from_left = moved_lane >= LANES - 2
    holds = jnp.where(lane % 4 < 2, moved_lane // 4, (moved_lane // 4 + 16) % 32)
    top = 0
    for n in range(count):
        height = ins[2 * n].shape[2]
        for p in range(2):
            for e in range(echoes):
                for s in range(2):
                    x = ins[2 * n + p][e, s].astype(jnp.float32)
                    for z in range(chips):
                        at = pl.ds(p * echoes + e, height, stride=2 * echoes)
                        turned[s, z, at, :] = x[:, z * LANES : (z + 1) * LANES]
        for k in range(chips):
            to = chip ^ k
            left_of, right_of = to - 1 + core, to + core
            has_left = (left_of >= 0).astype(jnp.float32)
            has_right = (right_of < chips).astype(jnp.float32)
            left_of, right_of = jnp.maximum(left_of, 0), jnp.minimum(right_of, chips - 1)
            edge = jnp.zeros((2 * echoes, LANES), jnp.float32)
            for r in range(height):
                at = pl.ds(r * 2 * echoes, 2 * echoes)
                moved = pltpu.roll(turned[1 - core, to, at, :], HALF, 1)
                outs[k][top + r] = jnp.where(in_place, turned[core, to, at, :], moved).astype(jnp.bfloat16)
                for s in range(2):
                    i = r + BLK * s
                    both = jnp.where(from_left, turned[s, left_of, at, :], turned[s, right_of, at, :])
                    edge = jnp.where(holds == i, pltpu.roll(both.astype(jnp.bfloat16), 4 * i + 2, 1).astype(jnp.float32), edge)
            edge = edge * jnp.where(lane % 4 < 2, has_left, has_right)
            outs[k][top + height] = pltpu.roll(edge, HALF * core, 1).astype(jnp.bfloat16)
        top += height + 1


def pack(pair, place, chunk, beyond, chips, edges):
    echoes, slices, height, cols = pair[0].shape
    block = lambda b: pl.BlockSpec((echoes, slices, BLK, cols), lambda _: (0, 0, b, 0))
    ins = [(a, block(b)) for b in chunk for a in pair]
    for a in beyond:
        half = lambda p: pl.BlockSpec((echoes,) + a.shape[1:], lambda _: (p, 0, 0, 0))
        ins += [(a, half(0)), (a, half(1))]
    count = len(ins) // 2
    rows = sum(spec.block_shape[2] + 1 for _, spec in ins[::2])
    shape = jax.ShapeDtypeStruct((rows, 2 * echoes, LANES), pair[0].dtype)
    out_shape = [shape] * chips
    extra = []
    if edges:
        extra = [(a, block(b)) for b in (0, height // BLK - 1) for a in pair]
        out_shape = out_shape + [jax.ShapeDtypeStruct((2 * echoes, slices, 2, cols), pair[0].dtype)] * 2
    ins = ins + extra
    zeros = lambda n: lambda _: (0,) * n
    return pl.pallas_call(
        functools.partial(pack_body, chips, count, len(extra)),
        grid=(1,),
        out_shape=out_shape,
        in_specs=[pl.BlockSpec(memory_space=pltpu.SMEM)] + [spec for _, spec in ins],
        out_specs=[pl.BlockSpec(o.shape, zeros(len(o.shape))) for o in out_shape],
        scratch_shapes=[pltpu.VMEM((2, chips, BLK * 2 * echoes, LANES), jnp.float32)],
        cost_estimate=pl.CostEstimate(
            flops=0, bytes_accessed=8 * echoes * slices * rows * cols, transcendentals=0
        ),
        compiler_params=pltpu.CompilerParams(vmem_limit_bytes=PACK_VMEM),
        name="pack",
    )(place, *[a for a, _ in ins])


def swap(a, axis, distance):
    count = lax.axis_size(axis)
    return lax.ppermute(a, axis, [(i, i ^ distance) for i in range(count)])


def even(count, most=RB):
    parts = pl.cdiv(count, most)
    at = [count * p // parts for p in range(parts + 1)]
    return [(a, b - a) for a, b in zip(at, at[1:])]


def fit_body(runs, counts, first, rows, ends, starts, place, kb_ref, gs_ref, vec_ref, *refs):
    total = sum(counts)
    arrays, out = refs[:total], refs[total + starts]
    lhs, lhs_h, turned, sb, v0b, w, v1b, sb_h, v0_h, lr_h, v1_h, result, sem = refs[total + starts + 1 :]
    sources, at = [], 0
    for n in counts:
        sources.append(arrays[at : at + n])
        at += n
    s = pl.program_id(0)
    at_left, at_right = (place[0] == 0) & (place[1] == 0), (place[0] == ends[0]) & (place[1] == 1)
    at_top, at_bottom = (place[2] == 0) & (first == 0), (place[2] == ends[1]) & (first + rows == out.shape[1])
    bins = gs_ref.shape[0]
    halves = [slice(0, LANES), slice(LANES, 2 * LANES)]
    main = slice(BLK, BLK + HALF)

    def gather(source, slot):
        return jnp.concatenate([ref[slot].astype(jnp.float32) for ref in source], axis=0)

    def turn(src, slot, to, u):
        turned[u, :, 0:E] = gather(src, slot).T
        for t in range(lhs.shape[0]):
            for k in range(HALF // BLK):
                pair = [turned[u, pl.ds(HALF * t + q, 8, stride=8), :][:, 0:E] for q in ORDER[2 * k : 2 * k + 2]]
                lhs[t, to, k * BLK : (k + 1) * BLK, :] = jnp.concatenate(pair, axis=0).astype(jnp.bfloat16)

    @pl.when(s == 0)
    def _():
        lhs_h[...] = jnp.zeros_like(lhs_h)
        for source, slot0, edge_slot, edge_row, to, length in runs:
            src = sources[source]
            full = length // TURN

            for t in range(length):
                turn(src, slot0 + t, to + t, t % TURN)
            turned[0, :, 0:E] = gather(src, edge_slot).T
            for t in range(lhs.shape[0]):
                i = BLK * t + edge_row
                for at, col in ((0, 4 * ((i + BLK) % 32) + 2), (1, 4 * ((i + BLK) % 32) + 3), (6, 4 * i), (7, 4 * i + 1)):
                    lhs_h[t, pl.ds(8 * to + at, length, stride=8), :] = turned[0, pl.ds(col, length, stride=4), :]

    step, keep, pull = vec_ref[0:1, :], vec_ref[1:2, :], vec_ref[2:3, :]
    sub = lax.broadcasted_iota(jnp.int32, (8, LANES), 0)

    def sides(v, outer):
        a, b = pltpu.roll(v[HALF - 8 :], 1, 0), pltpu.roll(v[0:8], 7, 0)
        c, d = pltpu.roll(outer, 1, 0), pltpu.roll(outer, 7, 0)
        left = jnp.concatenate([jnp.where(sub == 0, c, a), v[HALF - 16 : HALF - 8]], axis=0)
        right = jnp.concatenate([v[8:16], jnp.where(sub == 7, d, b)], axis=0)
        beside = jnp.where(sub == 0, a, b) + jnp.where(sub == 0, d, c)
        return left.astype(jnp.bfloat16), right.astype(jnp.bfloat16), beside

    x = lhs_h[s][:, 0:E].astype(jnp.bfloat16)
    b = jnp.dot(x, kb_ref[0:E], preferred_element_type=jnp.float32) * step
    sb_h[...] = b.reshape(rows + 4, 8, bins)
    v0_h[...] = jnp.maximum(b, 0.0).reshape(rows + 4, 8, bins)

    for j, height in even(rows + 4):
        x = lhs[s, j : j + height].reshape(height * HALF, E)
        b = jnp.dot(x, kb_ref[0:E], preferred_element_type=jnp.float32)
        for r in range(height):
            for h in halves:
                t = b[r * HALF : (r + 1) * HALF, h] * step[:, h]
                sb[j + r, :, h] = t
                v = jnp.maximum(t, 0.0)
                left, right, beside = sides(v, v0_h[j + r, :, h])
                v0b[j + r, 0:BLK, h] = left
                v0b[j + r, main, h] = v.astype(jnp.bfloat16)
                v0b[j + r, BLK + HALF :, h] = right
                lr_h[j + r, :, h] = beside

    x = v0_h[1 : rows + 3].astype(jnp.bfloat16).reshape((rows + 2) * 8, bins)
    g = jnp.dot(x, gs_ref[...], preferred_element_type=jnp.float32).reshape(rows + 2, 8, bins)
    at = lax.broadcasted_iota(jnp.int32, (1, 8, bins), 1)
    inside = jnp.where(((at == 0) & (at_right)) | ((at == 7) & at_left), 0.0, 1.0)
    near = lr_h[1 : rows + 3] + (v0_h[0 : rows + 2] + v0_h[2 : rows + 4])
    v = v0_h[1 : rows + 3] * keep + sb_h[1 : rows + 3] + pull * near - g
    v1_h[1 : rows + 3] = jnp.maximum(v, 0.0) * inside

    def around(ref, j, h):
        near = (ref[j, 0:HALF, h] + ref[j, 2 * BLK :, h]) + (ref[j - 1, main, h] + ref[j + 1, main, h])
        return near.astype(jnp.float32)

    for j, height in even(rows + 2):
        j += 1
        x = v0b[j : j + height, main].reshape(height * HALF, bins)
        g = jnp.dot(x, gs_ref[...], preferred_element_type=jnp.float32)
        for r in range(height):
            for h in halves:
                b = sb[j + r, :, h]
                near = around(v0b, j + r, h)
                v = jnp.maximum(b * (1.0 + keep[:, h]), b) + pull[:, h] * near - g[r * HALF : (r + 1) * HALF, h]
                v = jnp.maximum(v, 0.0)
                w[j + r, :, h] = v * keep[:, h] + b
                left, right, _unused = sides(v, v1_h[j + r, :, h])
                v1b[j + r, 0:BLK, h] = left
                v1b[j + r, main, h] = v.astype(jnp.bfloat16)
                v1b[j + r, BLK + HALF :, h] = right
    for outside, j in ((at_top, 1), (at_bottom, rows + 2)):

        @pl.when(outside)
        def _():
            v1b[j] = jnp.zeros_like(v1b[j])

    for i, height in even(rows):
        j = 2 + i
        x = v1b[j : j + height, main].reshape(height * HALF, bins)
        g = jnp.dot(x, gs_ref[...], preferred_element_type=jnp.float32)
        for r in range(height):
            for n, h in enumerate(halves):
                v = w[j + r, :, h] + pull[:, h] * around(v1b, j + r, h) - g[r * HALF : (r + 1) * HALF, h]
                v = jnp.maximum(v, 0.0)
                for t, q in enumerate(ORDER):
                    result[s, n, i + r, pl.ds(q, 8, stride=8), :] = v[8 * t : 8 * t + 8]
        for n, h in enumerate(halves):
            pltpu.make_async_copy(
                result.at[s, n, pl.ds(i, height)], out.at[s, pl.ds(first + i, height), :, h], sem.at[s]
            ).start()

    @pl.when(s == pl.num_programs(0) - 1)
    def _():
        for t in range(result.shape[0]):
            for n, h in enumerate(halves):
                pltpu.make_async_copy(result.at[t, n], out.at[t, pl.ds(first, rows), :, h], sem.at[t]).wait()


def fit(first, last, ends, shape, place, parts, sources, before):
    rows = last - first
    runs = []
    for to, row in enumerate(range(first - 2, last + 2)):
        for n, (_, where) in enumerate(sources):
            if row in where:
                slot, edge_slot, edge_row = where[row]
                prev = runs[-1] if runs else None
                if prev and prev[0] == n and prev[2] == edge_slot and prev[1] + prev[5] == slot:
                    runs[-1] = prev[:5] + (prev[5] + 1,)
                else:
                    runs.append((n, slot, edge_slot, edge_row, to, 1))
                break
        else:
            raise ValueError("row")
    keep = sorted({run[0] for run in runs})
    runs = [(keep.index(run[0]),) + run[1:] for run in runs]
    groups = [sources[n][0] for n in keep]
    arrays = [a for group in groups for a in group]
    counts = [len(group) for group in groups]
    slices = shape[0]
    whole = pl.BlockSpec(memory_space=pl.ANY)
    bins = shape[-1]
    tiles = lambda n, width, dtype: pltpu.VMEM((n, width, bins), dtype)
    specs = [pl.BlockSpec(a.shape, lambda s: (0, 0, 0)) for a in arrays]
    voxels = slices * rows * HALF
    started = [] if before is None else [before]
    return pl.pallas_call(
        functools.partial(fit_body, runs, counts, first, rows, ends, len(started)),
        grid=(slices,),
        out_shape=jax.ShapeDtypeStruct(shape, jnp.float32),
        in_specs=[pl.BlockSpec(memory_space=pltpu.SMEM)]
        + [pl.BlockSpec(p.shape, lambda s: (0, 0)) for p in parts]
        + specs
        + [whole] * len(started),
        out_specs=whole,
        scratch_shapes=[
            pltpu.VMEM((slices, rows + 4, HALF, E), jnp.bfloat16),
            pltpu.VMEM((slices, (rows + 4) * 8, LANES), jnp.float32),
            pltpu.VMEM((TURN, LANES, LANES), jnp.float32),
            tiles(rows + 4, HALF, jnp.float32),
            tiles(rows + 4, HALF + 2 * BLK, jnp.bfloat16),
            tiles(rows + 4, HALF, jnp.float32),
            tiles(rows + 4, HALF + 2 * BLK, jnp.bfloat16),
            tiles(rows + 4, 8, jnp.float32),
            tiles(rows + 4, 8, jnp.float32),
            tiles(rows + 4, 8, jnp.float32),
            tiles(rows + 4, 8, jnp.float32),
            pltpu.VMEM((slices, 2, rows, HALF, LANES), jnp.float32),
            pltpu.SemaphoreType.DMA((slices,)),
        ],
        input_output_aliases={4 + len(arrays): 0} if started else {},
        cost_estimate=pl.CostEstimate(
            flops=voxels * 256 * 2 * (2 * 256 + 64), bytes_accessed=voxels * 256 * 4, transcendentals=0
        ),
        compiler_params=pltpu.CompilerParams(vmem_limit_bytes=FIT_VMEM),
        name="fit",
    )(place, *parts, *arrays, *started)


def per_device(images, rates, smoothing):
    echoes, slices, height, _ = images.shape
    chips = lax.axis_size("gy") // 2
    ends = lax.axis_size("gx") - 1
    me = lax.axis_index("gy").astype(jnp.int32)
    place = jnp.stack([me // 2, me % 2, lax.axis_index("gx").astype(jnp.int32)])

    pair = (images, swap(images, "gy", 1))
    packs, wheres = [], []
    for n, chunk in enumerate(CHUNKS):
        inner = [b for b in chunk if 0 <= b < height // BLK]
        blocks = [[b * BLK + r for r in range(BLK)] for b in inner]
        extra = []
        if -1 in chunk:
            extra.append(above)
            blocks.append([-2, -1])
        if height // BLK in chunk:
            extra.append(below)
            blocks.append([height, height + 1])
        packed = pack(pair, place, inner, extra, chips, n == 0)
        if n == 0:
            top, bottom = packed[chips:]
            above = lax.ppermute(bottom, "gx", [(i, i + 1) for i in range(ends)])
            below = lax.ppermute(top, "gx", [(i + 1, i) for i in range(ends)])
            parts = kernel_parts(rates, smoothing, place, echoes, packed[0])
        packs.append(packed[:chips])
        where, at = {}, 0
        for block in blocks:
            for r, row in enumerate(block):
                where[row] = (at + r, at + len(block), r)
            at += len(block) + 1
        wheres.append(where)

    arrived = []
    for n in range(len(CHUNKS)):
        if n == 1:
            packs[1:], parts, arrived[0][1] = lax.optimization_barrier((packs[1:], parts, arrived[0][1]))
        elif n > 1:
            packs[n], arrived[n - 1] = lax.optimization_barrier((packs[n], arrived[n - 1]))
        moved = {k: swap(packs[n][k], "gy", 2 * k) for k in range(chips - 1, 0, -1)}
        arrived.append([packs[n][0]] + [moved[k] for k in range(1, chips)])

    shape = (slices, height, HALF, rates.shape[0])
    out = None
    for first, last, used in SEGS:
        out = fit(first, last, (chips - 1, ends), shape, place, parts, list(zip(arrived[:used], wheres)), out)
    return out


def solution(mesh):
    in_specs = (P("gy", None, "gx", None), P(), P())
    out_specs = P(None, "gx", "gy", None)
    return jax.shard_map(per_device, mesh=mesh, in_specs=in_specs, out_specs=out_specs, check_vma=False)
```

```python
import functools

import jax
import jax.numpy as jnp
from jax import lax
from jax.experimental import pallas as pl
from jax.experimental.pallas import tpu as pltpu
from jax.sharding import PartitionSpec as P

E = 64
BLK = 16
LANES = 128
HALF = 64
ORDER = (0, 4, 1, 5, 2, 6, 3, 7)
RB = 4
TURN = 16
PACK_VMEM, FIT_VMEM = 64 * 2**20, 64 * 2**20

CHUNKS = ((2, 3, 4), (5, 6, 7, 8), (0, 1, -1))
SEGS = ((36, 76, 1), (76, 128, 2), (0, 36, 3))


def parts_body(echoes, place, rates, smoothing, _, kb_ref, gs_ref, vec_ref):
    chip, core = place[0], place[1]
    pos = lax.broadcasted_iota(jnp.int32, (E, 1), 0)
    raw = jnp.exp(-10.0 * (pos.astype(jnp.float32) + 1.0) * rates[...])
    norm = jnp.sqrt(jnp.sum(raw * raw, axis=0, keepdims=True))
    kernel = raw / norm
    gram = lax.dot_general(
        kernel,
        kernel,
        (((0,), (0,)), ((), ())),
        precision=lax.Precision.HIGHEST,
        preferred_element_type=jnp.float32,
    )
    rowsum = jnp.sum(gram, axis=0, keepdims=True)
    lam = smoothing[...] * rowsum
    step = 1.0 / (rowsum + 8.0 * lam)
    owner = 2 * (chip ^ (pos // (2 * echoes))) + (core ^ (pos // echoes % 2))
    times = 10.0 * ((owner * echoes + pos % echoes).astype(jnp.float32) + 1.0)
    kb_ref[...] = (jnp.exp(-times * rates[...]) / norm).astype(jnp.bfloat16)
    gs_ref[...] = (gram * step).astype(jnp.bfloat16)
    pull = step * lam
    vec_ref[0:1, :] = step
    vec_ref[1:2, :] = 1.0 - 4.0 * pull
    vec_ref[2:3, :] = pull


def kernel_parts(rates, smoothing, place, echoes, later):
    bins = rates.shape[0]
    whole = pl.BlockSpec(memory_space=pltpu.VMEM)
    return pl.pallas_call(
        functools.partial(parts_body, echoes),
        out_shape=[
            jax.ShapeDtypeStruct((E, bins), jnp.bfloat16),
            jax.ShapeDtypeStruct((bins, bins), jnp.bfloat16),
            jax.ShapeDtypeStruct((8, bins), jnp.float32),
        ],
        in_specs=[pl.BlockSpec(memory_space=pltpu.SMEM), whole, whole, pl.BlockSpec(memory_space=pl.ANY)],
        out_specs=[whole] * 3,
        compiler_params=pltpu.CompilerParams(vmem_limit_bytes=PACK_VMEM),
        name="parts",
    )(place, rates[None, :], smoothing[None, :], later)


def pack_body(chips, count, ends, place, *refs):
    ins, refs = refs[: 2 * count], refs[2 * count :]
    ends, outs, turned = refs[:ends], refs[ends:-1], refs[-1]
    echoes = ins[0].shape[0]
    chip, core = place[0], place[1]
    if ends:
        for p in range(2):
            outs[chips][p * echoes : (p + 1) * echoes] = ends[p][:, :, 0:2]
            outs[chips + 1][p * echoes : (p + 1) * echoes] = ends[2 + p][:, :, BLK - 2 : BLK]
    lane = lax.broadcasted_iota(jnp.int32, (2 * echoes, LANES), 1)
    in_place = (lane < HALF) == (core == 0)
    moved_lane = (lane + HALF * core) % LANES
    from_left = moved_lane >= LANES - 2
    holds = jnp.where(lane % 4 < 2, moved_lane // 4, (moved_lane // 4 + 16) % 32)
    top = 0
    for n in range(count):
        height = ins[2 * n].shape[2]
        for p in range(2):
            for e in range(echoes):
                for s in range(2):
                    x = ins[2 * n + p][e, s].astype(jnp.float32)
                    for z in range(chips):
                        at = pl.ds(p * echoes + e, height, stride=2 * echoes)
                        turned[s, z, at, :] = x[:, z * LANES : (z + 1) * LANES]
        for k in range(chips):
            to = chip ^ k
            left_of, right_of = to - 1 + core, to + core
            has_left = (left_of >= 0).astype(jnp.float32)
            has_right = (right_of < chips).astype(jnp.float32)
            left_of, right_of = jnp.maximum(left_of, 0), jnp.minimum(right_of, chips - 1)
            edge = jnp.zeros((2 * echoes, LANES), jnp.float32)
            for r in range(height):
                at = pl.ds(r * 2 * echoes, 2 * echoes)
                moved = pltpu.roll(turned[1 - core, to, at, :], HALF, 1)
                outs[k][top + r] = jnp.where(in_place, turned[core, to, at, :], moved).astype(jnp.bfloat16)
                for s in range(2):
                    i = r + BLK * s
                    both = jnp.where(from_left, turned[s, left_of, at, :], turned[s, right_of, at, :])
                    edge = jnp.where(holds == i, pltpu.roll(both.astype(jnp.bfloat16), 4 * i + 2, 1).astype(jnp.float32), edge)
            edge = edge * jnp.where(lane % 4 < 2, has_left, has_right)
            outs[k][top + height] = pltpu.roll(edge, HALF * core, 1).astype(jnp.bfloat16)
        top += height + 1


def pack(pair, place, chunk, beyond, chips, edges):
    echoes, slices, height, cols = pair[0].shape
    block = lambda b: pl.BlockSpec((echoes, slices, BLK, cols), lambda _: (0, 0, b, 0))
    ins = [(a, block(b)) for b in chunk for a in pair]
    for a in beyond:
        half = lambda p: pl.BlockSpec((echoes,) + a.shape[1:], lambda _: (p, 0, 0, 0))
        ins += [(a, half(0)), (a, half(1))]
    count = len(ins) // 2
    rows = sum(spec.block_shape[2] + 1 for _, spec in ins[::2])
    shape = jax.ShapeDtypeStruct((rows, 2 * echoes, LANES), pair[0].dtype)
    out_shape = [shape] * chips
    extra = []
    if edges:
        extra = [(a, block(b)) for b in (0, height // BLK - 1) for a in pair]
        out_shape = out_shape + [jax.ShapeDtypeStruct((2 * echoes, slices, 2, cols), pair[0].dtype)] * 2
    ins = ins + extra
    zeros = lambda n: lambda _: (0,) * n
    return pl.pallas_call(
        functools.partial(pack_body, chips, count, len(extra)),
        grid=(1,),
        out_shape=out_shape,
        in_specs=[pl.BlockSpec(memory_space=pltpu.SMEM)] + [spec for _, spec in ins],
        out_specs=[pl.BlockSpec(o.shape, zeros(len(o.shape))) for o in out_shape],
        scratch_shapes=[pltpu.VMEM((2, chips, BLK * 2 * echoes, LANES), jnp.float32)],
        cost_estimate=pl.CostEstimate(
            flops=0, bytes_accessed=8 * echoes * slices * rows * cols, transcendentals=0
        ),
        compiler_params=pltpu.CompilerParams(vmem_limit_bytes=PACK_VMEM),
        name="pack",
    )(place, *[a for a, _ in ins])


def swap(a, axis, distance):
    count = lax.axis_size(axis)
    return lax.ppermute(a, axis, [(i, i ^ distance) for i in range(count)])


def even(count, most=RB):
    parts = pl.cdiv(count, most)
    at = [count * p // parts for p in range(parts + 1)]
    return [(a, b - a) for a, b in zip(at, at[1:])]


def fit_body(runs, counts, first, rows, ends, starts, place, kb_ref, gs_ref, vec_ref, *refs):
    total = sum(counts)
    arrays, out = refs[:total], refs[total + starts]
    lhs, lhs_h, turned, sb, v0b, w, v1b, sb_h, v0_h, lr_h, v1_h, result, sem = refs[total + starts + 1 :]
    sources, at = [], 0
    for n in counts:
        sources.append(arrays[at : at + n])
        at += n
    s = pl.program_id(0)
    at_left, at_right = (place[0] == 0) & (place[1] == 0), (place[0] == ends[0]) & (place[1] == 1)
    at_top, at_bottom = (place[2] == 0) & (first == 0), (place[2] == ends[1]) & (first + rows == out.shape[1])
    bins = gs_ref.shape[0]
    halves = [slice(0, LANES), slice(LANES, 2 * LANES)]
    main = slice(BLK, BLK + HALF)

    def gather(source, slot):
        return jnp.concatenate([ref[slot].astype(jnp.float32) for ref in source], axis=0)

    def turn(src, slot, to, u):
        turned[u, :, 0:E] = gather(src, slot).T
        for t in range(lhs.shape[0]):
            for k in range(HALF // BLK):
                pair = [turned[u, pl.ds(HALF * t + q, 8, stride=8), :][:, 0:E] for q in ORDER[2 * k : 2 * k + 2]]
                lhs[t, to, k * BLK : (k + 1) * BLK, :] = jnp.concatenate(pair, axis=0).astype(jnp.bfloat16)

    @pl.when(s == 0)
    def _():
        lhs_h[...] = jnp.zeros_like(lhs_h)
        for source, slot0, edge_slot, edge_row, to, length in runs:
            src = sources[source]
            full = length // TURN

            for t in range(length):
                turn(src, slot0 + t, to + t, t % TURN)
            turned[0, :, 0:E] = gather(src, edge_slot).T
            for t in range(lhs.shape[0]):
                i = BLK * t + edge_row
                for at, col in ((0, 4 * ((i + BLK) % 32) + 2), (1, 4 * ((i + BLK) % 32) + 3), (6, 4 * i), (7, 4 * i + 1)):
                    lhs_h[t, pl.ds(8 * to + at, length, stride=8), :] = turned[0, pl.ds(col, length, stride=4), :]

    step, keep, pull = vec_ref[0:1, :], vec_ref[1:2, :], vec_ref[2:3, :]
    sub = lax.broadcasted_iota(jnp.int32, (8, LANES), 0)

    def sides(v, outer):
        a, b = pltpu.roll(v[HALF - 8 :], 1, 0), pltpu.roll(v[0:8], 7, 0)
        c, d = pltpu.roll(outer, 1, 0), pltpu.roll(outer, 7, 0)
        left = jnp.concatenate([jnp.where(sub == 0, c, a), v[HALF - 16 : HALF - 8]], axis=0)
        right = jnp.concatenate([v[8:16], jnp.where(sub == 7, d, b)], axis=0)
        beside = jnp.where(sub == 0, a, b) + jnp.where(sub == 0, d, c)
        return left.astype(jnp.bfloat16), right.astype(jnp.bfloat16), beside

    x = lhs_h[s][:, 0:E].astype(jnp.bfloat16)
    b = jnp.dot(x, kb_ref[0:E], preferred_element_type=jnp.float32) * step
    sb_h[...] = b.reshape(rows + 4, 8, bins)
    v0_h[...] = jnp.maximum(b, 0.0).reshape(rows + 4, 8, bins)

    for j, height in even(rows + 4):
        x = lhs[s, j : j + height].reshape(height * HALF, E)
        b = jnp.dot(x, kb_ref[0:E], preferred_element_type=jnp.float32)
        for r in range(height):
            for h in halves:
                t = b[r * HALF : (r + 1) * HALF, h] * step[:, h]
                sb[j + r, :, h] = t
                v = jnp.maximum(t, 0.0)
                left, right, beside = sides(v, v0_h[j + r, :, h])
                v0b[j + r, 0:BLK, h] = left
                v0b[j + r, main, h] = v.astype(jnp.bfloat16)
                v0b[j + r, BLK + HALF :, h] = right
                lr_h[j + r, :, h] = beside

    x = v0_h[1 : rows + 3].astype(jnp.bfloat16).reshape((rows + 2) * 8, bins)
    g = jnp.dot(x, gs_ref[...], preferred_element_type=jnp.float32).reshape(rows + 2, 8, bins)
    at = lax.broadcasted_iota(jnp.int32, (1, 8, bins), 1)
    inside = jnp.where(((at == 0) & (at_right)) | ((at == 7) & at_left), 0.0, 1.0)
    near = lr_h[1 : rows + 3] + (v0_h[0 : rows + 2] + v0_h[2 : rows + 4])
    v = v0_h[1 : rows + 3] * keep + sb_h[1 : rows + 3] + pull * near - g
    v1_h[1 : rows + 3] = jnp.maximum(v, 0.0) * inside

    def around(ref, j, h):
        near = (ref[j, 0:HALF, h] + ref[j, 2 * BLK :, h]) + (ref[j - 1, main, h] + ref[j + 1, main, h])
        return near.astype(jnp.float32)

    for j, height in even(rows + 2):
        j += 1
        x = v0b[j : j + height, main].reshape(height * HALF, bins)
        g = jnp.dot(x, gs_ref[...], preferred_element_type=jnp.float32)
        for r in range(height):
            for h in halves:
                b = sb[j + r, :, h]
                near = around(v0b, j + r, h)
                v = jnp.maximum(b * (1.0 + keep[:, h]), b) + pull[:, h] * near - g[r * HALF : (r + 1) * HALF, h]
                v = jnp.maximum(v, 0.0)
                w[j + r, :, h] = v * keep[:, h] + b
                left, right, _unused = sides(v, v1_h[j + r, :, h])
                v1b[j + r, 0:BLK, h] = left
                v1b[j + r, main, h] = v.astype(jnp.bfloat16)
                v1b[j + r, BLK + HALF :, h] = right
    for outside, j in ((at_top, 1), (at_bottom, rows + 2)):

        @pl.when(outside)
        def _():
            v1b[j] = jnp.zeros_like(v1b[j])

    for i, height in even(rows):
        j = 2 + i
        x = v1b[j : j + height, main].reshape(height * HALF, bins)
        g = jnp.dot(x, gs_ref[...], preferred_element_type=jnp.float32)
        for r in range(height):
            for n, h in enumerate(halves):
                v = w[j + r, :, h] + pull[:, h] * around(v1b, j + r, h) - g[r * HALF : (r + 1) * HALF, h]
                v = jnp.maximum(v, 0.0)
                for t, q in enumerate(ORDER):
                    result[s, n, i + r, pl.ds(q, 8, stride=8), :] = v[8 * t : 8 * t + 8]
        for n, h in enumerate(halves):
            pltpu.make_async_copy(
                result.at[s, n, pl.ds(i, height)], out.at[s, pl.ds(first + i, height), :, h], sem.at[s]
            ).start()

    @pl.when(s == pl.num_programs(0) - 1)
    def _():
        for t in range(result.shape[0]):
            for n, h in enumerate(halves):
                pltpu.make_async_copy(result.at[t, n], out.at[t, pl.ds(first, rows), :, h], sem.at[t]).wait()


def fit(first, last, ends, shape, place, parts, sources, before):
    rows = last - first
    runs = []
    for to, row in enumerate(range(first - 2, last + 2)):
        for n, (_, where) in enumerate(sources):
            if row in where:
                slot, edge_slot, edge_row = where[row]
                prev = runs[-1] if runs else None
                if prev and prev[0] == n and prev[2] == edge_slot and prev[1] + prev[5] == slot:
                    runs[-1] = prev[:5] + (prev[5] + 1,)
                else:
                    runs.append((n, slot, edge_slot, edge_row, to, 1))
                break
        else:
            raise ValueError("row")
    keep = sorted({run[0] for run in runs})
    runs = [(keep.index(run[0]),) + run[1:] for run in runs]
    groups = [sources[n][0] for n in keep]
    arrays = [a for group in groups for a in group]
    counts = [len(group) for group in groups]
    slices = shape[0]
    whole = pl.BlockSpec(memory_space=pl.ANY)
    bins = shape[-1]
    tiles = lambda n, width, dtype: pltpu.VMEM((n, width, bins), dtype)
    specs = [pl.BlockSpec(a.shape, lambda s: (0, 0, 0)) for a in arrays]
    voxels = slices * rows * HALF
    started = [] if before is None else [before]
    return pl.pallas_call(
        functools.partial(fit_body, runs, counts, first, rows, ends, len(started)),
        grid=(slices,),
        out_shape=jax.ShapeDtypeStruct(shape, jnp.float32),
        in_specs=[pl.BlockSpec(memory_space=pltpu.SMEM)]
        + [pl.BlockSpec(p.shape, lambda s: (0, 0)) for p in parts]
        + specs
        + [whole] * len(started),
        out_specs=whole,
        scratch_shapes=[
            pltpu.VMEM((slices, rows + 4, HALF, E), jnp.bfloat16),
            pltpu.VMEM((slices, (rows + 4) * 8, LANES), jnp.float32),
            pltpu.VMEM((TURN, LANES, LANES), jnp.float32),
            tiles(rows + 4, HALF, jnp.float32),
            tiles(rows + 4, HALF + 2 * BLK, jnp.bfloat16),
            tiles(rows + 4, HALF, jnp.float32),
            tiles(rows + 4, HALF + 2 * BLK, jnp.bfloat16),
            tiles(rows + 4, 8, jnp.float32),
            tiles(rows + 4, 8, jnp.float32),
            tiles(rows + 4, 8, jnp.float32),
            tiles(rows + 4, 8, jnp.float32),
            pltpu.VMEM((slices, 2, rows, HALF, LANES), jnp.float32),
            pltpu.SemaphoreType.DMA((slices,)),
        ],
        input_output_aliases={4 + len(arrays): 0} if started else {},
        cost_estimate=pl.CostEstimate(
            flops=voxels * 256 * 2 * (2 * 256 + 64), bytes_accessed=voxels * 256 * 4, transcendentals=0
        ),
        compiler_params=pltpu.CompilerParams(vmem_limit_bytes=FIT_VMEM),
        name="fit",
    )(place, *parts, *arrays, *started)


def per_device(images, rates, smoothing):
    echoes, slices, height, _ = images.shape
    chips = lax.axis_size("gy") // 2
    ends = lax.axis_size("gx") - 1
    me = lax.axis_index("gy").astype(jnp.int32)
    place = jnp.stack([me // 2, me % 2, lax.axis_index("gx").astype(jnp.int32)])

    pair = (images, swap(images, "gy", 1))
    arrived, wheres = [], []
    for n, chunk in enumerate(CHUNKS):
        inner = [b for b in chunk if 0 <= b < height // BLK]
        blocks = [[b * BLK + r for r in range(BLK)] for b in inner]
        extra = []
        if -1 in chunk:
            extra.append(above)
            blocks.append([-2, -1])
        if height // BLK in chunk:
            extra.append(below)
            blocks.append([height, height + 1])
        if n > 1:
            pair, arrived[n - 2][-1] = lax.optimization_barrier((pair, arrived[n - 2][-1]))
        packed = pack(pair, place, inner, extra, chips, n == 0)
        if n == 0:
            top, bottom = packed[chips:]
            above = lax.ppermute(bottom, "gx", [(i, i + 1) for i in range(ends)])
            below = lax.ppermute(top, "gx", [(i + 1, i) for i in range(ends)])
            parts = kernel_parts(rates, smoothing, place, echoes, packed[0])
        elif n == 1:
            packed, parts, above, arrived[0][1] = lax.optimization_barrier((packed, parts, above, arrived[0][1]))
        else:
            packed, arrived[n - 1] = lax.optimization_barrier((packed, arrived[n - 1]))
        moved = {k: swap(packed[k], "gy", 2 * k) for k in range(chips - 1, 0, -1)}
        arrived.append([packed[0]] + [moved[k] for k in range(1, chips)])
        where, at = {}, 0
        for block in blocks:
            for r, row in enumerate(block):
                where[row] = (at + r, at + len(block), r)
            at += len(block) + 1
        wheres.append(where)

    shape = (slices, height, HALF, rates.shape[0])
    out = None
    for first, last, used in SEGS:
        out = fit(first, last, (chips - 1, ends), shape, place, parts, list(zip(arrived[:used], wheres)), out)
    return out


def solution(mesh):
    in_specs = (P("gy", None, "gx", None), P(), P())
    out_specs = P(None, "gx", "gy", None)
    return jax.shard_map(per_device, mesh=mesh, in_specs=in_specs, out_specs=out_specs, check_vma=False)
```

```python
import functools

import jax
import jax.numpy as jnp
from jax import lax
from jax.experimental import pallas as pl
from jax.experimental.pallas import tpu as pltpu
from jax.sharding import PartitionSpec as P

E = 64
BLK = 16
LANES = 128
HALF = 64
ORDER = (0, 4, 1, 5, 2, 6, 3, 7)
RB = 4
TURN = 16
PACK_VMEM, FIT_VMEM = 64 * 2**20, 64 * 2**20

CHUNKS = ((2, 3, 4), (5, 6, 7, 8), (0, 1, -1))
SEGS = ((36, 76, 1), (76, 128, 2), (0, 36, 3))


def parts_body(echoes, place, rates, smoothing, _, kb_ref, gs_ref, vec_ref):
    chip, core = place[0], place[1]
    pos = lax.broadcasted_iota(jnp.int32, (E, 1), 0)
    raw = jnp.exp(-10.0 * (pos.astype(jnp.float32) + 1.0) * rates[...])
    norm = jnp.sqrt(jnp.sum(raw * raw, axis=0, keepdims=True))
    kernel = raw / norm
    gram = lax.dot_general(
        kernel,
        kernel,
        (((0,), (0,)), ((), ())),
        precision=lax.Precision.HIGHEST,
        preferred_element_type=jnp.float32,
    )
    rowsum = jnp.sum(gram, axis=0, keepdims=True)
    lam = smoothing[...] * rowsum
    step = 1.0 / (rowsum + 8.0 * lam)
    owner = 2 * (chip ^ (pos // (2 * echoes))) + (core ^ (pos // echoes % 2))
    times = 10.0 * ((owner * echoes + pos % echoes).astype(jnp.float32) + 1.0)
    kb_ref[...] = (jnp.exp(-times * rates[...]) / norm).astype(jnp.bfloat16)
    gs_ref[...] = (gram * step).astype(jnp.bfloat16)
    pull = step * lam
    vec_ref[0:1, :] = step
    vec_ref[1:2, :] = 1.0 - 4.0 * pull
    vec_ref[2:3, :] = pull


def kernel_parts(rates, smoothing, place, echoes, later):
    bins = rates.shape[0]
    whole = pl.BlockSpec(memory_space=pltpu.VMEM)
    return pl.pallas_call(
        functools.partial(parts_body, echoes),
        out_shape=[
            jax.ShapeDtypeStruct((E, bins), jnp.bfloat16),
            jax.ShapeDtypeStruct((bins, bins), jnp.bfloat16),
            jax.ShapeDtypeStruct((8, bins), jnp.float32),
        ],
        in_specs=[pl.BlockSpec(memory_space=pltpu.SMEM), whole, whole, pl.BlockSpec(memory_space=pl.ANY)],
        out_specs=[whole] * 3,
        compiler_params=pltpu.CompilerParams(vmem_limit_bytes=PACK_VMEM),
        name="parts",
    )(place, rates[None, :], smoothing[None, :], later)


def pack_body(chips, count, ends, place, *refs):
    ins, refs = refs[: 2 * count], refs[2 * count :]
    ends, outs, turned = refs[:ends], refs[ends:-1], refs[-1]
    echoes = ins[0].shape[0]
    chip, core = place[0], place[1]
    if ends:
        for p in range(2):
            outs[chips][p * echoes : (p + 1) * echoes] = ends[p][:, :, 0:2]
            outs[chips + 1][p * echoes : (p + 1) * echoes] = ends[2 + p][:, :, BLK - 2 : BLK]
    lane = lax.broadcasted_iota(jnp.int32, (2 * echoes, LANES), 1)
    in_place = (lane < HALF) == (core == 0)
    moved_lane = (lane + HALF * core) % LANES
    from_left = moved_lane >= LANES - 2
    holds = jnp.where(lane % 4 < 2, moved_lane // 4, (moved_lane // 4 + 16) % 32)
    top = 0
    for n in range(count):
        height = ins[2 * n].shape[2]
        for p in range(2):
            for e in range(echoes):
                for s in range(2):
                    x = ins[2 * n + p][e, s].astype(jnp.float32)
                    for z in range(chips):
                        at = pl.ds(p * echoes + e, height, stride=2 * echoes)
                        turned[s, z, at, :] = x[:, z * LANES : (z + 1) * LANES]
        for k in range(chips):
            to = chip ^ k
            left_of, right_of = to - 1 + core, to + core
            has_left = (left_of >= 0).astype(jnp.float32)
            has_right = (right_of < chips).astype(jnp.float32)
            left_of, right_of = jnp.maximum(left_of, 0), jnp.minimum(right_of, chips - 1)
            edge = jnp.zeros((2 * echoes, LANES), jnp.float32)
            for r in range(height):
                at = pl.ds(r * 2 * echoes, 2 * echoes)
                moved = pltpu.roll(turned[1 - core, to, at, :], HALF, 1)
                outs[k][top + r] = jnp.where(in_place, turned[core, to, at, :], moved).astype(jnp.bfloat16)
                for s in range(2):
                    i = r + BLK * s
                    both = jnp.where(from_left, turned[s, left_of, at, :], turned[s, right_of, at, :])
                    edge = jnp.where(holds == i, pltpu.roll(both.astype(jnp.bfloat16), 4 * i + 2, 1).astype(jnp.float32), edge)
            edge = edge * jnp.where(lane % 4 < 2, has_left, has_right)
            outs[k][top + height] = pltpu.roll(edge, HALF * core, 1).astype(jnp.bfloat16)
        top += height + 1


def pack(pair, place, chunk, beyond, chips, edges):
    echoes, slices, height, cols = pair[0].shape
    block = lambda b: pl.BlockSpec((echoes, slices, BLK, cols), lambda _: (0, 0, b, 0))
    ins = [(a, block(b)) for b in chunk for a in pair]
    for a in beyond:
        half = lambda p: pl.BlockSpec((echoes,) + a.shape[1:], lambda _: (p, 0, 0, 0))
        ins += [(a, half(0)), (a, half(1))]
    count = len(ins) // 2
    rows = sum(spec.block_shape[2] + 1 for _, spec in ins[::2])
    shape = jax.ShapeDtypeStruct((rows, 2 * echoes, LANES), pair[0].dtype)
    out_shape = [shape] * chips
    extra = []
    if edges:
        extra = [(a, block(b)) for b in (0, height // BLK - 1) for a in pair]
        out_shape = out_shape + [jax.ShapeDtypeStruct((2 * echoes, slices, 2, cols), pair[0].dtype)] * 2
    ins = ins + extra
    zeros = lambda n: lambda _: (0,) * n
    return pl.pallas_call(
        functools.partial(pack_body, chips, count, len(extra)),
        grid=(1,),
        out_shape=out_shape,
        in_specs=[pl.BlockSpec(memory_space=pltpu.SMEM)] + [spec for _, spec in ins],
        out_specs=[pl.BlockSpec(o.shape, zeros(len(o.shape))) for o in out_shape],
        scratch_shapes=[pltpu.VMEM((2, chips, BLK * 2 * echoes, LANES), jnp.float32)],
        cost_estimate=pl.CostEstimate(
            flops=0, bytes_accessed=8 * echoes * slices * rows * cols, transcendentals=0
        ),
        compiler_params=pltpu.CompilerParams(vmem_limit_bytes=PACK_VMEM),
        name="pack",
    )(place, *[a for a, _ in ins])


def swap(a, axis, distance):
    count = lax.axis_size(axis)
    return lax.ppermute(a, axis, [(i, i ^ distance) for i in range(count)])


def even(count, most=RB):
    parts = pl.cdiv(count, most)
    at = [count * p // parts for p in range(parts + 1)]
    return [(a, b - a) for a, b in zip(at, at[1:])]


def fit_body(runs, counts, first, rows, ends, starts, place, kb_ref, gs_ref, vec_ref, *refs):
    total = sum(counts)
    arrays, out = refs[:total], refs[total + starts]
    lhs, lhs_h, turned, sb, v0b, w, v1b, sb_h, v0_h, lr_h, v1_h, result, sem = refs[total + starts + 1 :]
    sources, at = [], 0
    for n in counts:
        sources.append(arrays[at : at + n])
        at += n
    s = pl.program_id(0)
    at_left, at_right = (place[0] == 0) & (place[1] == 0), (place[0] == ends[0]) & (place[1] == 1)
    at_top, at_bottom = (place[2] == 0) & (first == 0), (place[2] == ends[1]) & (first + rows == out.shape[1])
    bins = gs_ref.shape[0]
    halves = [slice(0, LANES), slice(LANES, 2 * LANES)]
    main = slice(BLK, BLK + HALF)

    def gather(source, slot):
        return jnp.concatenate([ref[slot].astype(jnp.float32) for ref in source], axis=0)

    def turn(src, slot, to, u):
        turned[u, :, 0:E] = gather(src, slot).T
        for t in range(lhs.shape[0]):
            for k in range(HALF // BLK):
                pair = [turned[u, pl.ds(HALF * t + q, 8, stride=8), :][:, 0:E] for q in ORDER[2 * k : 2 * k + 2]]
                lhs[t, to, k * BLK : (k + 1) * BLK, :] = jnp.concatenate(pair, axis=0).astype(jnp.bfloat16)

    @pl.when(s == 0)
    def _():
        lhs_h[...] = jnp.zeros_like(lhs_h)
        for source, slot0, edge_slot, edge_row, to, length in runs:
            src = sources[source]
            full = length // TURN

            for t in range(length):
                turn(src, slot0 + t, to + t, t % TURN)
            turned[0, :, 0:E] = gather(src, edge_slot).T
            for t in range(lhs.shape[0]):
                i = BLK * t + edge_row
                for at, col in ((0, 4 * ((i + BLK) % 32) + 2), (1, 4 * ((i + BLK) % 32) + 3), (6, 4 * i), (7, 4 * i + 1)):
                    lhs_h[t, pl.ds(8 * to + at, length, stride=8), :] = turned[0, pl.ds(col, length, stride=4), :]

    step, keep, pull = vec_ref[0:1, :], vec_ref[1:2, :], vec_ref[2:3, :]
    sub = lax.broadcasted_iota(jnp.int32, (8, LANES), 0)

    def sides(v, outer):
        a, b = pltpu.roll(v[HALF - 8 :], 1, 0), pltpu.roll(v[0:8], 7, 0)
        c, d = pltpu.roll(outer, 1, 0), pltpu.roll(outer, 7, 0)
        left = jnp.concatenate([jnp.where(sub == 0, c, a), v[HALF - 16 : HALF - 8]], axis=0)
        right = jnp.concatenate([v[8:16], jnp.where(sub == 7, d, b)], axis=0)
        beside = jnp.where(sub == 0, a, b) + jnp.where(sub == 0, d, c)
        return left.astype(jnp.bfloat16), right.astype(jnp.bfloat16), beside

    x = lhs_h[s, 0 : (rows + 4) * 8][:, 0:E].astype(jnp.bfloat16)
    b = jnp.dot(x, kb_ref[0:E], preferred_element_type=jnp.float32) * step
    sb_h[...] = b.reshape(rows + 4, 8, bins)
    v0_h[...] = jnp.maximum(b, 0.0).reshape(rows + 4, 8, bins)

    for j, height in even(rows + 4):
        x = lhs[s, j : j + height].reshape(height * HALF, E)
        b = jnp.dot(x, kb_ref[0:E], preferred_element_type=jnp.float32)
        for r in range(height):
            for h in halves:
                t = b[r * HALF : (r + 1) * HALF, h] * step[:, h]
                sb[j + r, :, h] = t
                v = jnp.maximum(t, 0.0)
                left, right, beside = sides(v, v0_h[j + r, :, h])
                v0b[j + r, 0:BLK, h] = left
                v0b[j + r, main, h] = v.astype(jnp.bfloat16)
                v0b[j + r, BLK + HALF :, h] = right
                lr_h[j + r, :, h] = beside

    x = v0_h[1 : rows + 3].astype(jnp.bfloat16).reshape((rows + 2) * 8, bins)
    g = jnp.dot(x, gs_ref[...], preferred_element_type=jnp.float32).reshape(rows + 2, 8, bins)
    at = lax.broadcasted_iota(jnp.int32, (1, 8, bins), 1)
    inside = jnp.where(((at == 0) & (at_right)) | ((at == 7) & at_left), 0.0, 1.0)
    near = lr_h[1 : rows + 3] + (v0_h[0 : rows + 2] + v0_h[2 : rows + 4])
    v = v0_h[1 : rows + 3] * keep + sb_h[1 : rows + 3] + pull * near - g
    v1_h[1 : rows + 3] = jnp.maximum(v, 0.0) * inside

    def around(ref, j, h):
        near = (ref[j, 0:HALF, h] + ref[j, 2 * BLK :, h]) + (ref[j - 1, main, h] + ref[j + 1, main, h])
        return near.astype(jnp.float32)

    for j, height in even(rows + 2):
        j += 1
        x = v0b[j : j + height, main].reshape(height * HALF, bins)
        g = jnp.dot(x, gs_ref[...], preferred_element_type=jnp.float32)
        for r in range(height):
            for h in halves:
                b = sb[j + r, :, h]
                near = around(v0b, j + r, h)
                v = jnp.maximum(b * (1.0 + keep[:, h]), b) + pull[:, h] * near - g[r * HALF : (r + 1) * HALF, h]
                v = jnp.maximum(v, 0.0)
                w[j + r, :, h] = v * keep[:, h] + b
                left, right, _unused = sides(v, v1_h[j + r, :, h])
                v1b[j + r, 0:BLK, h] = left
                v1b[j + r, main, h] = v.astype(jnp.bfloat16)
                v1b[j + r, BLK + HALF :, h] = right
    for outside, j in ((at_top, 1), (at_bottom, rows + 2)):

        @pl.when(outside)
        def _():
            v1b[j] = jnp.zeros_like(v1b[j])

    for i, height in even(rows):
        j = 2 + i
        x = v1b[j : j + height, main].reshape(height * HALF, bins)
        g = jnp.dot(x, gs_ref[...], preferred_element_type=jnp.float32)
        for r in range(height):
            for n, h in enumerate(halves):
                v = w[j + r, :, h] + pull[:, h] * around(v1b, j + r, h) - g[r * HALF : (r + 1) * HALF, h]
                v = jnp.maximum(v, 0.0)
                for t, q in enumerate(ORDER):
                    result[s, n, i + r, pl.ds(q, 8, stride=8), :] = v[8 * t : 8 * t + 8]
        for n, h in enumerate(halves):
            pltpu.make_async_copy(
                result.at[s, n, pl.ds(i, height)], out.at[s, pl.ds(first + i, height), :, h], sem.at[s]
            ).start()

    @pl.when(s == pl.num_programs(0) - 1)
    def _():
        for t in range(result.shape[0]):
            for n, h in enumerate(halves):
                pltpu.make_async_copy(result.at[t, n], out.at[t, pl.ds(first, rows), :, h], sem.at[t]).wait()


def fit(first, last, ends, shape, place, parts, sources, before):
    rows = last - first
    runs = []
    for to, row in enumerate(range(first - 2, last + 2)):
        for n, (_, where) in enumerate(sources):
            if row in where:
                slot, edge_slot, edge_row = where[row]
                prev = runs[-1] if runs else None
                if prev and prev[0] == n and prev[2] == edge_slot and prev[1] + prev[5] == slot:
                    runs[-1] = prev[:5] + (prev[5] + 1,)
                else:
                    runs.append((n, slot, edge_slot, edge_row, to, 1))
                break
        else:
            raise ValueError("row")
    keep = sorted({run[0] for run in runs})
    runs = [(keep.index(run[0]),) + run[1:] for run in runs]
    groups = [sources[n][0] for n in keep]
    arrays = [a for group in groups for a in group]
    counts = [len(group) for group in groups]
    slices = shape[0]
    whole = pl.BlockSpec(memory_space=pl.ANY)
    bins = shape[-1]
    tiles = lambda n, width, dtype: pltpu.VMEM((n, width, bins), dtype)
    specs = [pl.BlockSpec(a.shape, lambda s: (0, 0, 0)) for a in arrays]
    voxels = slices * rows * HALF
    started = [] if before is None else [before]
    return pl.pallas_call(
        functools.partial(fit_body, runs, counts, first, rows, ends, len(started)),
        grid=(slices,),
        out_shape=jax.ShapeDtypeStruct(shape, jnp.float32),
        in_specs=[pl.BlockSpec(memory_space=pltpu.SMEM)]
        + [pl.BlockSpec(p.shape, lambda s: (0, 0)) for p in parts]
        + specs
        + [whole] * len(started),
        out_specs=whole,
        scratch_shapes=[
            pltpu.VMEM((slices, rows + 4, HALF, E), jnp.bfloat16),
            pltpu.VMEM((slices, (rows + 12) * 8, LANES), jnp.float32),
            pltpu.VMEM((TURN, LANES, LANES), jnp.float32),
            tiles(rows + 4, HALF, jnp.float32),
            tiles(rows + 4, HALF + 2 * BLK, jnp.bfloat16),
            tiles(rows + 4, HALF, jnp.float32),
            tiles(rows + 4, HALF + 2 * BLK, jnp.bfloat16),
            tiles(rows + 4, 8, jnp.float32),
            tiles(rows + 4, 8, jnp.float32),
            tiles(rows + 4, 8, jnp.float32),
            tiles(rows + 4, 8, jnp.float32),
            pltpu.VMEM((slices, 2, rows, HALF, LANES), jnp.float32),
            pltpu.SemaphoreType.DMA((slices,)),
        ],
        input_output_aliases={4 + len(arrays): 0} if started else {},
        cost_estimate=pl.CostEstimate(
            flops=voxels * 256 * 2 * (2 * 256 + 64), bytes_accessed=voxels * 256 * 4, transcendentals=0
        ),
        compiler_params=pltpu.CompilerParams(vmem_limit_bytes=FIT_VMEM),
        name="fit",
    )(place, *parts, *arrays, *started)


def per_device(images, rates, smoothing):
    echoes, slices, height, _ = images.shape
    chips = lax.axis_size("gy") // 2
    ends = lax.axis_size("gx") - 1
    me = lax.axis_index("gy").astype(jnp.int32)
    place = jnp.stack([me // 2, me % 2, lax.axis_index("gx").astype(jnp.int32)])

    pair = (images, swap(images, "gy", 1))
    arrived, wheres = [], []
    for n, chunk in enumerate(CHUNKS):
        inner = [b for b in chunk if 0 <= b < height // BLK]
        blocks = [[b * BLK + r for r in range(BLK)] for b in inner]
        extra = []
        if -1 in chunk:
            extra.append(above)
            blocks.append([-2, -1])
        if height // BLK in chunk:
            extra.append(below)
            blocks.append([height, height + 1])
        if n > 1:
            pair, arrived[n - 2][-1] = lax.optimization_barrier((pair, arrived[n - 2][-1]))
        packed = pack(pair, place, inner, extra, chips, n == 0)
        if n == 0:
            top, bottom = packed[chips:]
            above = lax.ppermute(bottom, "gx", [(i, i + 1) for i in range(ends)])
            below = lax.ppermute(top, "gx", [(i + 1, i) for i in range(ends)])
            parts = kernel_parts(rates, smoothing, place, echoes, packed[0])
        elif n == 1:
            packed, parts, above, arrived[0][1] = lax.optimization_barrier((packed, parts, above, arrived[0][1]))
        else:
            packed, arrived[n - 1] = lax.optimization_barrier((packed, arrived[n - 1]))
        moved = {k: swap(packed[k], "gy", 2 * k) for k in range(chips - 1, 0, -1)}
        arrived.append([packed[0]] + [moved[k] for k in range(1, chips)])
        where, at = {}, 0
        for block in blocks:
            for r, row in enumerate(block):
                where[row] = (at + r, at + len(block), r)
            at += len(block) + 1
        wheres.append(where)

    shape = (slices, height, HALF, rates.shape[0])
    out = None
    for first, last, used in SEGS:
        out = fit(first, last, (chips - 1, ends), shape, place, parts, list(zip(arrived[:used], wheres)), out)
    return out


def solution(mesh):
    in_specs = (P("gy", None, "gx", None), P(), P())
    out_specs = P(None, "gx", "gy", None)
    return jax.shard_map(per_device, mesh=mesh, in_specs=in_specs, out_specs=out_specs, check_vma=False)
```
